256 devices in a mesh: blk: 16 (over y, z_lo, core), head: 16 (over x, z_hi).
Axes of the slice: x: 4, y: 4, z: 8 (z_hi: 4, z_lo: 2; z = z_hi * 2 + z_lo), core: 2. Of those that a mesh axis runs over, the one named last changes fastest.
Arguments:
- query: bfloat16 [16384, 2, 1024], P(('blk', 'head')), may hold values from -6.59375 to 6.59375
- key_in: bfloat16 [16384, 2, 1024], P(('blk', 'head')), may hold values from -6.59375 to 6.59375
- value: bfloat16 [16384, 2, 1024], P(('blk', 'head')), may hold values from -6 to 6
- output: bfloat16 [16384, 2, 1024], P(('blk', 'head')), may hold values from -2 to 2
- grad_out: bfloat16 [16384, 2, 1024], P(('blk', 'head')), may hold values from -192 to 192
- log_sum_exp: float32 [16, 2, 16384], P(None, None, ('blk', 'head')), as said below
Outputs:
- grad_query: bfloat16 [16384, 2, 1024], P(('blk', 'head'))
- grad_key: bfloat16 [16384, 2, 1024], P(('blk', 'head'))
- grad_value: bfloat16 [16384, 2, 1024], P(('blk', 'head'))
The draws below stay inside these ranges and needn't reach their ends.
Inputs may be any that keep to these rules, and one draw needn't show every extreme that they name: `log_sum_exp`: each entry lies between log(16384) + 0.5 and log(16384) + 1.5.
All inputs are finite; a program needn't handle non-finite values.
Results may differ from the reference program's by a relative error of at most 0.0054.
Values may be sent and summed in bfloat16 or wider, within the bound.
A program may use at most 192 MiB of HBM per device.

```python
import math
import jax
import jax.numpy as jnp
from jax import lax

HEADS = 16
HD = 64
SEQS = 2
WIDTH = 1024
FRAMES = 16384


def draw_log_sum_exp(key, part):
    key = jax.random.fold_in(key, 7)
    base_level = jnp.log(jnp.float32(FRAMES))
    offsets = jax.random.uniform(key, (HEADS, SEQS, FRAMES), jnp.float32, 0.75, 1.5)
    return base_level + offsets


def levels(own_key, extent, split, least, top_value):
    factor_of = 1.0
    for dim, blocks in split:
        steps = jax.random.uniform(jax.random.fold_in(jax.random.fold_in(own_key, 6), dim), (blocks,), jnp.float32, least / len(split), top_value / len(split))
        factor_of = factor_of * jnp.repeat(jnp.exp(steps), extent[dim] // blocks).reshape((-1,) + (1,) * (len(extent) - 1 - dim))
    return factor_of


def gaussian(own_key, extent, scale, most, split=(), kind=jnp.bfloat16):
    level = levels(own_key, extent, split, -0.22, 0.18) if split else 1.0
    result = jax.random.normal(own_key, extent, jnp.float32) * scale * level
    return jnp.minimum(jnp.maximum(result, -most), most).astype(kind)


def setup_inputs(seed: int = 0) -> dict:
    key_list = jax.random.split(jax.random.key(seed), 7)
    return {
        "query": gaussian(key_list[0], (FRAMES, SEQS, WIDTH), 1.1, 6.59375, ((0, 256),)),
        "key_in": gaussian(key_list[1], (FRAMES, SEQS, WIDTH), 1.1, 6.59375, ((0, 256),)),
        "value": gaussian(key_list[2], (FRAMES, SEQS, WIDTH), 1.0, 6.0, ((0, 256),)),
        "output": gaussian(key_list[3], (FRAMES, SEQS, WIDTH), 0.3, 2.0, ((0, 256),)),
        "grad_out": gaussian(key_list[4], (FRAMES, SEQS, WIDTH), 32.0, 192.0, ((0, 256),)),
        "log_sum_exp": draw_log_sum_exp(jax.random.fold_in(key_list[6], 71), 0),
    }


def head_grads(queries, keys_all, values_all, grad_rows, lse_rows, dot_rows):
    block_rows = math.gcd(FRAMES, 1024)
    score_scale = HD ** -0.5
    blocks_total = FRAMES // block_rows

    def visit_block(carry, block_index):
        grad_keys, grad_values = carry
        first_row = block_index * block_rows
        query_blk = lax.dynamic_slice_in_dim(queries, first_row, block_rows, 0)
        out_blk = lax.dynamic_slice_in_dim(grad_rows, first_row, block_rows, 0)
        lse_blk = lax.dynamic_slice_in_dim(lse_rows, first_row, block_rows, 0)
        dot_blk = lax.dynamic_slice_in_dim(dot_rows, first_row, block_rows, 0)
        scores = jnp.dot(query_blk, keys_all.T, preferred_element_type=jnp.float32) * score_scale
        attn_probs = jnp.exp(scores - lse_blk[:, None])
        grad_values = grad_values + jnp.dot(attn_probs.astype(jnp.bfloat16).T, out_blk, preferred_element_type=jnp.float32)
        grad_probs = jnp.dot(out_blk, values_all.T, preferred_element_type=jnp.float32)
        grad_scores = (attn_probs * (grad_probs - dot_blk[:, None]) * score_scale).astype(jnp.bfloat16)
        grad_queries = jnp.dot(grad_scores, keys_all, preferred_element_type=jnp.float32)
        grad_keys = grad_keys + jnp.dot(grad_scores.T, query_blk, preferred_element_type=jnp.float32)
        return (grad_keys, grad_values), grad_queries

    zeros_init = jnp.zeros((FRAMES, HD), jnp.float32)
    (grad_keys, grad_values), grad_queries = lax.scan(visit_block, (zeros_init, zeros_init), jnp.arange(blocks_total, dtype=jnp.int32))
    return grad_queries.reshape(FRAMES, HD), grad_keys, grad_values


def split_heads(matrix):
    return matrix.reshape(FRAMES, SEQS, HEADS, HD).transpose(1, 2, 0, 3).reshape(SEQS * HEADS, FRAMES, HD)


def join_heads(stacked):
    return stacked.reshape(SEQS, HEADS, FRAMES, HD).transpose(2, 0, 1, 3).reshape(FRAMES, SEQS, HEADS * HD).astype(jnp.bfloat16)


def reference(query, key_in, value, output, grad_out, log_sum_exp):
    products = output.astype(jnp.float32).reshape(FRAMES, SEQS, HEADS, HD) * grad_out.astype(jnp.float32).reshape(FRAMES, SEQS, HEADS, HD)
    row_dot = jnp.sum(products, axis=3).transpose(1, 2, 0).reshape(SEQS * HEADS, FRAMES)
    lse_flat = log_sum_exp.transpose(1, 0, 2).reshape(SEQS * HEADS, FRAMES)

    def per_head(operands):
        return head_grads(*operands)

    grad_q, grad_k, grad_v = lax.map(per_head, (split_heads(query), split_heads(key_in), split_heads(value), split_heads(grad_out), lse_flat, row_dot))
    return join_heads(grad_q), join_heads(grad_k), join_heads(grad_v)
```

```python
import math
import jax
import jax.numpy as jnp
from jax import lax
from jax.experimental import pallas as pl
from jax.experimental.pallas import tpu as pltpu
from jax.sharding import PartitionSpec as P

BF, F32 = jnp.bfloat16, jnp.float32
MESH = pl.DeviceIdType.MESH
NT = (((1,), (1,)), ((), ()))
TN = (((0,), (0,)), ((), ()))
LOG2E = math.log2(math.e)
SCALE = 0.125
ROWS = 1024
SLOT = 64


def iota(shape, dim):
    return lax.broadcasted_iota(jnp.int32, shape, dim)


def low_half(rows):
    return iota((rows, 128), 1) < 64


def roll_half(tile):
    return pltpu.roll(tile, 64, 1)


def order_rows(transposed):
    shape = (128, 128)
    here, there = (iota(shape, 1), iota(shape, 0)) if transposed else (iota(shape, 0), iota(shape, 1))
    return jnp.where(there == 2 * lax.rem(here, 64) + lax.div(here, 64), 1.0, 0.0).astype(BF)


def place(high):
    return jnp.where(iota((64, 128), 1) == iota((64, 128), 0) + (64 if high else 0), 1.0, 0.0).astype(BF)


def kernel(
    q_ref, k_ref, v_ref, o_ref, g_ref, lse_ref, dq_ref, dk_ref, dv_ref,
    sq, sk, sa, qbuf, kbuf, ra, aux, kz, vz, kt, dqt, dka, dva,
    sdq, rdq, skv, rkv, oq, okv, iq, ikv,
    in_send, in_recv, ag_send, ag_recv, ax_send, ax_recv, dq_send, dq_recv,
    kx_send, kx_recv, dx_send, dx_recv, out_send, out_recv,
):
    blk, head = lax.axis_index("blk"), lax.axis_index("head")
    my_y, my_zl, my_c = lax.div(blk, 4), lax.rem(lax.div(blk, 2), 2), lax.rem(blk, 2)
    my_x, my_zh = lax.div(head, 4), lax.rem(head, 4)
    my_pair = my_x * 8 + my_y * 2 + my_zl

    def device(x, y, zl, zh, c):
        return (y * 4 + zl * 2 + c, x * 4 + zh)

    def offset(n):
        oy = lax.rem(lax.div(n, 2), 4)
        return lax.rem(lax.div(n, 8) + oy, 4), oy, lax.rem(n, 2)

    def ahead(n):
        ox, oy, ol = offset(n)
        return lax.rem(my_x + ox, 4), lax.rem(my_y + oy, 4), lax.rem(my_zl + ol, 2)

    def behind(n):
        ox, oy, ol = offset(n)
        return lax.rem(my_x + 4 - ox, 4), lax.rem(my_y + 4 - oy, 4), lax.rem(my_zl + 2 - ol, 2)

    def ring(distance):
        return device(my_x, my_y, my_zl, lax.rem(my_zh + distance, 4), my_c)

    partner = device(my_x, my_y, my_zl, my_zh, 1 - my_c)

    def send(src, dst, send_sem, recv_sem, target):
        return pltpu.make_async_remote_copy(
            src_ref=src, dst_ref=dst, send_sem=send_sem, recv_sem=recv_sem, device_id=target, device_id_type=MESH
        )

    def wait(ref, sem):
        pltpu.make_async_copy(ref, ref, sem).wait()

    barrier = pltpu.get_barrier_semaphore()

    def greet(n, c):
        x, y, zl = ahead(n)
        pl.semaphore_signal(barrier, inc=1, device_id=device(x, y, zl, my_zh, my_c), device_id_type=MESH)
        return c

    lax.fori_loop(1, 32, greet, 0)
    for target in (partner, ring(1), ring(2), ring(3)):
        pl.semaphore_signal(barrier, inc=1, device_id=target, device_id_type=MESH)

    to_seq = order_rows(False)

    def by_seq(ref):
        return jnp.dot(to_seq, ref[...], preferred_element_type=F32)

    def pack(low, high, dst):
        for t in range(8):
            a, b = low[:, t * 128:(t + 1) * 128], high[:, t * 128:(t + 1) * 128]
            even = jnp.where(low_half(128), a, roll_half(b)).astype(BF)
            odd = jnp.where(low_half(128), roll_half(a), b).astype(BF)
            for s in range(2):
                dst[4 * t + s] = even[s * 64:(s + 1) * 64]
                dst[4 * t + 2 + s] = odd[s * 64:(s + 1) * 64]

    grad_rows = by_seq(g_ref)
    pack(by_seq(q_ref), grad_rows, sq)
    rest = by_seq(o_ref) * grad_rows
    heads_of = jnp.where(iota((16, 1024), 0) == lax.div(iota((16, 1024), 1), 64), 1.0, 0.0).astype(BF)
    dots = jnp.zeros((16, 128), F32)
    for _ in range(3):
        part = rest.astype(BF)
        rest = rest - part.astype(F32)
        dots = dots + lax.dot_general(heads_of, part, NT, preferred_element_type=F32)
    dots_rolled = roll_half(dots)
    for h in range(16):
        for s in range(2):
            sa[2 * h + s, :, 0:64] = lse_ref[h, s:s + 1, :] * LOG2E
            sa[2 * h + s, :, 64:128] = (dots if s else dots_rolled)[h:h + 1, 64:128]
    pl.semaphore_wait(barrier, 35)

    def send_queries(n, c):
        x, y, zl = ahead(n)
        pair, target = x * 8 + y * 2 + zl, device(x, y, zl, my_zh, my_c)
        half, row = lax.div(n, 16), pl.multiple_of(lax.rem(n, 16) * SLOT, SLOT)
        send(sa.at[pair], ra.at[n], in_send.at[0], in_recv.at[half], target).start()
        send(sq.at[pair], qbuf.at[7 * half, pl.ds(row, SLOT)], in_send.at[1], in_recv.at[2 + half], target).start()
        return c

    def send_keys(n, c):
        x, y, zl = ahead(n)
        pair, target = x * 8 + y * 2 + zl, device(x, y, zl, my_zh, my_c)
        half, row = lax.div(n, 16), pl.multiple_of(lax.rem(n, 16) * SLOT, SLOT)
        send(sk.at[pair], kbuf.at[half, pl.ds(row, SLOT)], in_send.at[2], in_recv.at[4 + half], target).start()
        return c

    lax.fori_loop(1, 16, send_queries, 0)
    pack(by_seq(k_ref), by_seq(v_ref), sk)
    lax.fori_loop(1, 32, send_keys, 0)
    lax.fori_loop(16, 32, send_queries, 0)
    ra[0] = sa[my_pair]
    qbuf[0, 0:SLOT] = sq[my_pair]
    kbuf[0, 0:SLOT] = sk[my_pair]
    dqt[...] = jnp.zeros_like(dqt)
    dka[...] = jnp.zeros_like(dka)
    dva[...] = jnp.zeros_like(dva)

    def queries_here(half):
        first = 0 if half else 1
        wait(ra.at[pl.ds(16 * half + first, 16 - first)], in_recv.at[half])
        wait(qbuf.at[7 * half, pl.ds(0, (16 - first) * SLOT)], in_recv.at[2 + half])
        for m in range(8):
            a, b = ra[16 * half + 2 * m], ra[16 * half + 2 * m + 1]
            aux[7 * half, 0:1, m * 128:(m + 1) * 128] = jnp.where(low_half(1), a, roll_half(b))
            aux[7 * half, 1:2, m * 128:(m + 1) * 128] = jnp.where(low_half(1), roll_half(a), b)

    def pass_chunk(src, dst, distance):
        target = ring(distance)
        for buf, ss, rs in ((qbuf, ag_send, ag_recv), (aux, ax_send, ax_recv)):
            send(buf.at[src], buf.at[dst], ss.at[dst], rs.at[dst], target).start()

    def chunk_here(i):
        wait(qbuf.at[i], ag_recv.at[i])
        wait(aux.at[i], ax_recv.at[i])

    def prepare_keys(j):
        both = kbuf[j]
        low = low_half(ROWS)
        zero = jnp.zeros_like(both)
        kz[j] = jnp.where(low, both, zero)
        vz[j] = jnp.where(low, zero, both)
        eye = jnp.where(iota((64, 128), 0) == iota((64, 128), 1), 1.0, 0.0).astype(BF)
        kt[j] = lax.dot_general(eye, both, NT, preferred_element_type=F32).astype(BF)

    def keys_here(j):
        if j < 2:
            first = 0 if j else 1
            wait(kbuf.at[j, pl.ds(0, (16 - first) * SLOT)], in_recv.at[4 + j])
            send(kbuf.at[j], kbuf.at[2 + j], kx_send.at[j], kx_recv.at[j], partner).start()
        else:
            wait(kbuf.at[j], kx_recv.at[j - 2])
        prepare_keys(j)

    def both_grads(j):
        return jnp.where(low_half(ROWS), dka[j] * SCALE, dva[j])

    def send_out(lo, hi, src, dst, which):
        def one(n, c):
            x, y, zl = behind(n)
            target = device(x, y, zl, my_zh, my_c)
            send(src.at[n], dst.at[my_pair], out_send.at[which], out_recv.at[which], target).start()
            return c

        lax.fori_loop(max(lo, 1), hi, one, 0)
        if lo == 0:
            dst[my_pair] = src[0]

    def finish_queries(half):
        parts = (3, 4, 6) if half else (1, 2, 5)
        total = dqt[7 * half]
        for i in parts:
            wait(rdq.at[i - 1], dq_recv.at[i])
            total = total + rdq[i - 1].astype(F32)
        low = (total * SCALE).astype(BF)
        a = lax.dot_general(low, place(False), TN, preferred_element_type=F32)
        b = lax.dot_general(low, place(True), TN, preferred_element_type=F32)
        for n in range(16):
            both = a[n * 64:n * 64 + 32] + b[n * 64 + 32:n * 64 + 64]
            oq[16 * half + n] = both.astype(BF)
        send_out(16 * half, 16 * half + 16, oq, iq, 0)

    def finish_keys(j):
        wait(rkv.at[j], dx_recv.at[j])
        total = (both_grads(j) + rkv[j].astype(F32)).astype(BF)
        for n in range(16):
            okv[16 * j + n] = total[n * 64:(n + 1) * 64]
        send_out(16 * j, 16 * j + 16, okv, ikv, 1)

    queries_here(0)
    pass_chunk(0, 1, 3)
    pass_chunk(0, 2, 1)
    keys_here(0)

    def turn(t, c):
        i = lax.div(t, 4)
        j = lax.rem(lax.rem(t, 4) + 2 * lax.div(i, 7), 4)

        @pl.when(t == 1)
        def _():
            keys_here(1)
            queries_here(1)
            pass_chunk(7, 3, 3)
            pass_chunk(7, 4, 1)

        @pl.when(t == 2)
        def _():
            keys_here(2)

        @pl.when(t == 3)
        def _():
            keys_here(3)

        @pl.when(t == 4)
        def _():
            chunk_here(1)
            pass_chunk(1, 5, 3)

        @pl.when(t == 8)
        def _():
            chunk_here(2)

        @pl.when(t == 12)
        def _():
            chunk_here(3)
            chunk_here(4)
            pass_chunk(4, 6, 1)

        @pl.when(t == 20)
        def _():
            chunk_here(5)

        @pl.when(t == 24)
        def _():
            chunk_here(6)

        @pl.when(t == 30)
        def _():
            finish_queries(0)

        rows = qbuf[i]
        scores = lax.dot_general(kz[j], rows, NT, preferred_element_type=F32)
        grad_probs = lax.dot_general(vz[j], rows, NT, preferred_element_type=F32)
        probs = jnp.exp2(scores * (SCALE * LOG2E) - aux[i, 0:1, :])
        grad_scores = (probs * (grad_probs - aux[i, 1:2, :])).astype(BF)
        dva[j] += jnp.dot(probs.astype(BF), rows, preferred_element_type=F32)
        dka[j] += jnp.dot(grad_scores, rows, preferred_element_type=F32)
        dqt[i] += jnp.dot(kt[j], grad_scores, preferred_element_type=F32)

        for i_done, distance in ((1, 1), (2, 3), (3, 1), (4, 3), (5, 2), (6, 2)):

            @pl.when(t == 4 * i_done + 3)
            def _():
                sdq[i_done - 1] = dqt[i_done].astype(BF)
                send(sdq.at[i_done - 1], rdq.at[i_done - 1], dq_send.at[i_done], dq_recv.at[i_done], ring(distance)).start()

        for half in range(2):

            @pl.when(t == 28 + half)
            def _():
                skv[half] = both_grads(2 + half).astype(BF)
                send(skv.at[half], rkv.at[half], dx_send.at[half], dx_recv.at[half], partner).start()

        @pl.when(t == 30)
        def _():
            finish_keys(0)

        return c

    lax.fori_loop(0, 32, turn, 0)
    finish_keys(1)
    finish_queries(1)

    wait(sa.at[pl.ds(0, 31)], in_send.at[0])
    wait(sq.at[pl.ds(0, 31)], in_send.at[1])
    wait(sk.at[pl.ds(0, 31)], in_send.at[2])
    for i in range(1, 7):
        wait(qbuf.at[i], ag_send.at[i])
        wait(aux.at[i], ax_send.at[i])
        wait(sdq.at[i - 1], dq_send.at[i])
    for j in range(2):
        wait(kbuf.at[j], kx_send.at[j])
        wait(skv.at[j], dx_send.at[j])
    wait(oq.at[pl.ds(0, 31)], out_send.at[0])
    wait(okv.at[pl.ds(0, 31)], out_send.at[1])

    to_frames = order_rows(True)

    def interleave(tiles):
        rows = jnp.concatenate([jnp.concatenate([tiles(s, t) for t in range(8)], 1) for s in range(2)], 0)
        return jnp.dot(to_frames, rows.astype(BF), preferred_element_type=F32).astype(BF)

    wait(ikv.at[pl.ds(0, 31)], out_recv.at[1])

    def key_tile(s, t):
        return jnp.where(low_half(64), ikv[4 * t + s].astype(F32), roll_half(ikv[4 * t + 2 + s].astype(F32)))

    def value_tile(s, t):
        return jnp.where(low_half(64), roll_half(ikv[4 * t + s].astype(F32)), ikv[4 * t + 2 + s].astype(F32))

    def query_tile(s, t):
        a, b = iq[4 * t + s].astype(F32), iq[4 * t + 2 + s].astype(F32)
        first = jnp.where(low_half(32), a, roll_half(b))
        second = jnp.where(low_half(32), roll_half(a), b)
        return jnp.concatenate([first, second], 0)

    dk_ref[...] = interleave(key_tile)
    dv_ref[...] = interleave(value_tile)
    wait(iq.at[pl.ds(0, 31)], out_recv.at[0])
    dq_ref[...] = interleave(query_tile)


def shards(query, key_in, value, output, grad_out, log_sum_exp):
    shape = query.shape
    flat = (shape[0] * shape[1], shape[2])
    arrays = [a.reshape(flat) for a in (query, key_in, value, output, grad_out)]
    dma = pltpu.SemaphoreType.DMA
    vmem = pl.BlockSpec(memory_space=pltpu.VMEM)
    grads = pl.pallas_call(
        kernel,
        out_shape=[jax.ShapeDtypeStruct(flat, BF)] * 3,
        in_specs=[vmem] * 6,
        out_specs=[vmem] * 3,
        scratch_shapes=[
            pltpu.VMEM((32, SLOT, 128), BF),
            pltpu.VMEM((32, SLOT, 128), BF),
            pltpu.VMEM((32, 1, 128), F32),
            pltpu.VMEM((8, ROWS, 128), BF),
            pltpu.VMEM((4, ROWS, 128), BF),
            pltpu.VMEM((32, 1, 128), F32),
            pltpu.VMEM((8, 2, ROWS), F32),
            pltpu.VMEM((4, ROWS, 128), BF),
            pltpu.VMEM((4, ROWS, 128), BF),
            pltpu.VMEM((4, 64, ROWS), BF),
            pltpu.VMEM((8, 64, ROWS), F32),
            pltpu.VMEM((4, ROWS, 128), F32),
            pltpu.VMEM((4, ROWS, 128), F32),
            pltpu.VMEM((6, 64, ROWS), BF),
            pltpu.VMEM((6, 64, ROWS), BF),
            pltpu.VMEM((2, ROWS, 128), BF),
            pltpu.VMEM((2, ROWS, 128), BF),
            pltpu.VMEM((32, 32, 128), BF),
            pltpu.VMEM((32, SLOT, 128), BF),
            pltpu.VMEM((32, 32, 128), BF),
            pltpu.VMEM((32, SLOT, 128), BF),
            dma((3,)), dma((6,)),
            dma((8,)), dma((8,)),
            dma((8,)), dma((8,)),
            dma((8,)), dma((8,)),
            dma((2,)), dma((2,)),
            dma((2,)), dma((2,)),
            dma((2,)), dma((2,)),
        ],
        compiler_params=pltpu.CompilerParams(
            collective_id=0, has_side_effects=True, vmem_limit_bytes=56 * 2**20
        ),
    )(*arrays, log_sum_exp)
    return tuple(g.reshape(shape) for g in grads)


def solution(mesh):
    rows = P(("blk", "head"), None, None)
    return jax.shard_map(
        shards,
        mesh=mesh,
        in_specs=(rows,) * 5 + (P(None, None, ("blk", "head")),),
        out_specs=(rows,) * 3,
        check_vma=False,
    )
```

```python
import math
import jax
import jax.numpy as jnp
from jax import lax
from jax.experimental import pallas as pl
from jax.experimental.pallas import tpu as pltpu
from jax.sharding import PartitionSpec as P

BF, F32 = jnp.bfloat16, jnp.float32
MESH = pl.DeviceIdType.MESH
NT = (((1,), (1,)), ((), ()))
TN = (((0,), (0,)), ((), ()))
LOG2E = math.log2(math.e)
SCALE = 0.125
ROWS = 1024
SLOT = 64


def iota(shape, dim):
    return lax.broadcasted_iota(jnp.int32, shape, dim)


def low_half(rows):
    return iota((rows, 128), 1) < 64


def roll_half(tile):
    return pltpu.roll(tile, 64, 1)


def order_rows(transposed):
    shape = (128, 128)
    here, there = (iota(shape, 1), iota(shape, 0)) if transposed else (iota(shape, 0), iota(shape, 1))
    return jnp.where(there == 2 * lax.rem(here, 64) + lax.div(here, 64), 1.0, 0.0).astype(BF)


def eye(n):
    return jnp.where(iota((n, n), 0) == iota((n, n), 1), 1.0, 0.0).astype(BF)


def kernel(
    q_ref, k_ref, v_ref, o_ref, g_ref, lse_ref, dq_ref, dk_ref, dv_ref,
    sq, sk, sa, qbuf, kbuf, ra, aux, qz, gz, qgt, kzt, vzt, dqa, dkt, dvt,
    sdq, rdq, skv, rkv, oq, okv, iq, ikv,
    in_send, in_recv, ag_send, ag_recv, ax_send, ax_recv, dq_send, dq_recv,
    kx_send, kx_recv, dx_send, dx_recv, out_send, out_recv,
):
    blk, head = lax.axis_index("blk"), lax.axis_index("head")
    my_y, my_zl, my_c = lax.div(blk, 4), lax.rem(lax.div(blk, 2), 2), lax.rem(blk, 2)
    my_x, my_zh = lax.div(head, 4), lax.rem(head, 4)
    my_pair = my_x * 8 + my_y * 2 + my_zl

    def device(x, y, zl, zh, c):
        return (y * 4 + zl * 2 + c, x * 4 + zh)

    def offset(n):
        oy = lax.rem(lax.div(n, 2), 4)
        return lax.rem(lax.div(n, 8) + oy, 4), oy, lax.rem(n, 2)

    def ahead(n):
        ox, oy, ol = offset(n)
        return lax.rem(my_x + ox, 4), lax.rem(my_y + oy, 4), lax.rem(my_zl + ol, 2)

    def behind(n):
        ox, oy, ol = offset(n)
        return lax.rem(my_x + 4 - ox, 4), lax.rem(my_y + 4 - oy, 4), lax.rem(my_zl + 2 - ol, 2)

    def ring(distance):
        return device(my_x, my_y, my_zl, lax.rem(my_zh + distance, 4), my_c)

    partner = device(my_x, my_y, my_zl, my_zh, 1 - my_c)

    def send(src, dst, send_sem, recv_sem, target):
        return pltpu.make_async_remote_copy(
            src_ref=src, dst_ref=dst, send_sem=send_sem, recv_sem=recv_sem, device_id=target, device_id_type=MESH
        )

    def wait(ref, sem):
        pltpu.make_async_copy(ref, ref, sem).wait()

    barrier = pltpu.get_barrier_semaphore()

    def greet(n, c):
        x, y, zl = ahead(n)
        pl.semaphore_signal(barrier, inc=1, device_id=device(x, y, zl, my_zh, my_c), device_id_type=MESH)
        return c

    lax.fori_loop(1, 32, greet, 0)
    for target in (partner, ring(1), ring(2), ring(3)):
        pl.semaphore_signal(barrier, inc=1, device_id=target, device_id_type=MESH)

    to_seq = order_rows(False)

    def by_seq(ref):
        return jnp.dot(to_seq, ref[...].reshape(128, 1024), preferred_element_type=F32)

    def pack(low, high, dst):
        for t in range(8):
            a, b = low[:, t * 128:(t + 1) * 128], high[:, t * 128:(t + 1) * 128]
            even = jnp.where(low_half(128), a, roll_half(b)).astype(BF)
            odd = jnp.where(low_half(128), roll_half(a), b).astype(BF)
            for s in range(2):
                dst[4 * t + s] = even[s * 64:(s + 1) * 64]
                dst[4 * t + 2 + s] = odd[s * 64:(s + 1) * 64]

    grad_rows = by_seq(g_ref)
    pack(by_seq(q_ref), grad_rows, sq)
    rest = by_seq(o_ref) * grad_rows
    heads_of = jnp.where(iota((16, 1024), 0) == lax.div(iota((16, 1024), 1), 64), 1.0, 0.0).astype(BF)
    dots = jnp.zeros((16, 128), F32)
    for _ in range(3):
        part = rest.astype(BF)
        rest = rest - part.astype(F32)
        dots = dots + lax.dot_general(heads_of, part, NT, preferred_element_type=F32)
    dots_rolled = roll_half(dots)
    for h in range(16):
        for s in range(2):
            sa[2 * h + s, :, 0:64] = lse_ref[h, s:s + 1, :] * (-1.0 / SCALE)
            sa[2 * h + s, :, 64:128] = -(dots if s else dots_rolled)[h:h + 1, 64:128]
    pl.semaphore_wait(barrier, 35)

    def send_queries(n, c):
        x, y, zl = ahead(n)
        pair, target = x * 8 + y * 2 + zl, device(x, y, zl, my_zh, my_c)
        half, row = lax.div(n, 16), pl.multiple_of(lax.rem(n, 16) * SLOT, SLOT)
        send(sa.at[pair], ra.at[n], in_send.at[0], in_recv.at[half], target).start()
        send(sq.at[pair], qbuf.at[7 * half, pl.ds(row, SLOT)], in_send.at[1], in_recv.at[2 + half], target).start()
        return c

    def send_keys(n, c):
        x, y, zl = ahead(n)
        pair, target = x * 8 + y * 2 + zl, device(x, y, zl, my_zh, my_c)
        half, row = lax.div(n, 16), pl.multiple_of(lax.rem(n, 16) * SLOT, SLOT)
        send(sk.at[pair], kbuf.at[half, pl.ds(row, SLOT)], in_send.at[2], in_recv.at[4 + half], target).start()
        return c

    lax.fori_loop(1, 16, send_queries, 0)
    pack(by_seq(k_ref), by_seq(v_ref), sk)
    lax.fori_loop(1, 16, send_keys, 0)
    ra[0] = sa[my_pair]
    qbuf[0, 0:SLOT] = sq[my_pair]
    kbuf[0, 0:SLOT] = sk[my_pair]
    dqa[...] = jnp.zeros_like(dqa)
    dkt[...] = jnp.zeros_like(dkt)
    dvt[...] = jnp.zeros_like(dvt)

    def queries_here(half):
        first = 0 if half else 1
        wait(ra.at[pl.ds(16 * half + first, 16 - first)], in_recv.at[half])
        wait(qbuf.at[7 * half, pl.ds(0, (16 - first) * SLOT)], in_recv.at[2 + half])
        for m in range(8):
            a, b = ra[16 * half + 2 * m], ra[16 * half + 2 * m + 1]
            aux[7 * half, 0:1, m * 128:(m + 1) * 128] = jnp.where(low_half(1), a, roll_half(b))
            aux[7 * half, 1:2, m * 128:(m + 1) * 128] = jnp.where(low_half(1), roll_half(a), b)

    def pass_chunk(src, dst, distance):
        target = ring(distance)
        for buf, ss, rs in ((qbuf, ag_send, ag_recv), (aux, ax_send, ax_recv)):
            send(buf.at[src], buf.at[dst], ss.at[dst], rs.at[dst], target).start()

    def chunk_here(i):
        wait(qbuf.at[i], ag_recv.at[i])
        wait(aux.at[i], ax_recv.at[i])

    def prepare_keys(j):
        turned = lax.dot_general(eye(128), kbuf[j], NT, preferred_element_type=F32)
        row = iota((128, ROWS), 0)
        ones = jnp.where(lax.rem(row, 64) < 3, 1.0, 0.0)
        kzt[j] = jnp.where(row < 64, turned, ones).astype(BF)
        vzt[j] = jnp.where(row < 64, ones, turned).astype(BF)

    def prepare_queries(i):
        rest, parts = aux[i], []
        for _ in range(3):
            parts.append(rest.astype(BF).astype(F32))
            rest = rest - parts[-1]
        parts = jnp.concatenate(parts + [jnp.zeros((10, ROWS), F32)], 0).astype(BF)
        row, lane = iota((16, 128), 0), iota((16, 128), 1)
        spot = 64 * (1 - lax.rem(row, 2)) + lax.div(row, 2)
        spare = jnp.where((lane == spot) & (row < 6), 1.0, 0.0).astype(BF)
        columns = lax.dot_general(parts, spare, TN, preferred_element_type=F32).astype(BF)
        both = qbuf[i]
        low = low_half(ROWS)
        qz[...] = jnp.where(low, both, columns)
        gz[...] = jnp.where(low, columns, both)
        qgt[...] = lax.dot_general(eye(128), both, NT, preferred_element_type=F32).astype(BF)

    def front(j):
        scores = jnp.dot(qz[...], kzt[j], preferred_element_type=F32)
        grad_probs = jnp.dot(gz[...], vzt[j], preferred_element_type=F32)
        probs = jnp.exp2(scores * (SCALE * LOG2E))
        return probs.astype(BF), (probs * grad_probs).astype(BF)

    def back(i, j, probs, grad_scores):
        dvt[j] += jnp.dot(qgt[64:128], probs, preferred_element_type=F32)
        dkt[j] += jnp.dot(qgt[0:64], grad_scores, preferred_element_type=F32)
        dqa[i] += jnp.dot(grad_scores, kbuf[j], preferred_element_type=F32)

    def keys_here(j):
        if j < 2:
            first = 0 if j else 1
            wait(kbuf.at[j, pl.ds(0, (16 - first) * SLOT)], in_recv.at[4 + j])
            send(kbuf.at[j], kbuf.at[2 + j], kx_send.at[j], kx_recv.at[j], partner).start()
        else:
            wait(kbuf.at[j], kx_recv.at[j - 2])
        prepare_keys(j)

    def both_grads(j):
        return jnp.concatenate([dkt[j] * SCALE, dvt[j]], 0)

    def packed_queries(i):
        return jnp.where(low_half(ROWS // 2), dqa[i, 0:ROWS // 2], roll_half(dqa[i, ROWS // 2:ROWS]))

    def send_out(lo, hi, src, dst, which):
        def one(n, c):
            x, y, zl = behind(n)
            target = device(x, y, zl, my_zh, my_c)
            send(src.at[n], dst.at[my_pair], out_send.at[which], out_recv.at[which], target).start()
            return c

        lax.fori_loop(max(lo, 1), hi, one, 0)
        if lo == 0:
            dst[my_pair] = src[0]

    def finish_queries(half):
        total = packed_queries(7 * half)
        for i in (3, 5, 6) if half else (1, 2, 4):
            wait(rdq.at[i - 1], dq_recv.at[i])
            total = total + rdq[i - 1].astype(F32)
        total = total * SCALE
        low = low_half(32)
        for n in range(8):
            a, b = total[n * 64:n * 64 + 32], total[n * 64 + 32:n * 64 + 64]
            oq[16 * half + n] = jnp.where(low, a, roll_half(b)).astype(BF)
            oq[16 * half + 8 + n] = jnp.where(low, roll_half(a), b).astype(BF)
        send_out(16 * half, 16 * half + 16, oq, iq, 0)

    def finish_keys(j):
        wait(rkv.at[j], dx_recv.at[j])
        total = (both_grads(j) + rkv[j].astype(F32)).astype(BF)
        total = lax.dot_general(total, eye(128), TN, preferred_element_type=F32).astype(BF)
        for n in range(16):
            okv[16 * j + n] = total[n * 64:(n + 1) * 64]
        send_out(16 * j, 16 * j + 16, okv, ikv, 1)

    queries_here(0)
    pass_chunk(0, 1, 3)
    pass_chunk(0, 2, 1)
    keys_here(0)
    lax.fori_loop(16, 32, send_keys, 0)

    def start_turn(t, c):
        i, r = 7 * lax.div(t, 4), lax.rem(t, 4)
        second = lax.div(t, 4)
        j = (1 - second) * (lax.div(r, 2) + 2 * lax.rem(r, 2)) + second * (r + 2)

        @pl.when(t == 0)
        def _():
            prepare_queries(0)

        @pl.when(t == 1)
        def _():
            lax.fori_loop(16, 32, send_queries, 0)
            keys_here(2)

        @pl.when(t == 2)
        def _():
            keys_here(1)

        @pl.when(t == 3)
        def _():
            keys_here(3)

        @pl.when(t == 4)
        def _():
            queries_here(1)
            pass_chunk(7, 3, 3)
            pass_chunk(7, 6, 1)
            prepare_queries(7)

        back(i, j, *front(j))
        return c

    lax.fori_loop(0, 6, start_turn, 0)

    def middle_turn(i, c):
        @pl.when(i == 1)
        def _():
            chunk_here(1)
            pass_chunk(1, 4, 3)

        @pl.when(i == 2)
        def _():
            chunk_here(2)

        @pl.when(i == 3)
        def _():
            chunk_here(3)
            chunk_here(6)
            pass_chunk(6, 5, 1)

        for late in (4, 5):

            @pl.when(i == late)
            def _():
                chunk_here(late)

        prepare_queries(i)
        now = front(0)
        for j in range(4):
            later = front(j + 1) if j < 3 else None
            back(i, j, *now)
            now = later
        sdq[i - 1] = packed_queries(i).astype(BF)

        for done, distance in ((1, 1), (2, 3), (3, 1), (4, 2), (5, 2), (6, 3)):

            @pl.when(i == done)
            def _():
                send(sdq.at[done - 1], rdq.at[done - 1], dq_send.at[done], dq_recv.at[done], ring(distance)).start()

        return c

    lax.fori_loop(1, 7, middle_turn, 0)
    for half in range(2):
        skv[half] = both_grads(2 + half).astype(BF)
        send(skv.at[half], rkv.at[half], dx_send.at[half], dx_recv.at[half], partner).start()
    prepare_queries(7)
    finish_queries(0)

    for j in range(2):
        back(7, j, *front(j))
        finish_keys(j)
    finish_queries(1)

    wait(sa.at[pl.ds(0, 31)], in_send.at[0])
    wait(sq.at[pl.ds(0, 31)], in_send.at[1])
    wait(sk.at[pl.ds(0, 31)], in_send.at[2])
    for i in range(1, 7):
        wait(qbuf.at[i], ag_send.at[i])
        wait(aux.at[i], ax_send.at[i])
        wait(sdq.at[i - 1], dq_send.at[i])
    for j in range(2):
        wait(kbuf.at[j], kx_send.at[j])
        wait(skv.at[j], dx_send.at[j])
    wait(oq.at[pl.ds(0, 31)], out_send.at[0])
    wait(okv.at[pl.ds(0, 31)], out_send.at[1])

    to_frames = order_rows(True)

    def interleave(tiles):
        rows = jnp.concatenate([jnp.concatenate([tiles(s, t) for t in range(8)], 1) for s in range(2)], 0)
        rows = jnp.dot(to_frames, rows.astype(BF), preferred_element_type=F32).astype(BF)
        return rows.reshape(64, 2, 1024)

    wait(ikv.at[pl.ds(0, 31)], out_recv.at[1])

    def key_tile(s, t):
        return jnp.where(low_half(64), ikv[4 * t + s].astype(F32), roll_half(ikv[4 * t + 2 + s].astype(F32)))

    def value_tile(s, t):
        return jnp.where(low_half(64), roll_half(ikv[4 * t + s].astype(F32)), ikv[4 * t + 2 + s].astype(F32))

    def query_tile(s, t):
        a, b = iq[4 * t + s].astype(F32), iq[4 * t + 2 + s].astype(F32)
        first = jnp.where(low_half(32), a, roll_half(b))
        second = jnp.where(low_half(32), roll_half(a), b)
        return jnp.concatenate([first, second], 0)

    dk_ref[...] = interleave(key_tile)
    dv_ref[...] = interleave(value_tile)
    wait(iq.at[pl.ds(0, 31)], out_recv.at[0])
    dq_ref[...] = interleave(query_tile)


def shards(query, key_in, value, output, grad_out, log_sum_exp):
    dma = pltpu.SemaphoreType.DMA
    vmem = pl.BlockSpec(memory_space=pltpu.VMEM)
    return pl.pallas_call(
        kernel,
        out_shape=[jax.ShapeDtypeStruct(query.shape, BF)] * 3,
        in_specs=[vmem] * 6,
        out_specs=[vmem] * 3,
        scratch_shapes=[
            pltpu.VMEM((32, SLOT, 128), BF),
            pltpu.VMEM((32, SLOT, 128), BF),
            pltpu.VMEM((32, 1, 128), F32),
            pltpu.VMEM((8, ROWS, 128), BF),
            pltpu.VMEM((4, ROWS, 128), BF),
            pltpu.VMEM((32, 1, 128), F32),
            pltpu.VMEM((8, 2, ROWS), F32),
            pltpu.VMEM((ROWS, 128), BF),
            pltpu.VMEM((ROWS, 128), BF),
            pltpu.VMEM((128, ROWS), BF),
            pltpu.VMEM((4, 128, ROWS), BF),
            pltpu.VMEM((4, 128, ROWS), BF),
            pltpu.VMEM((8, ROWS, 128), F32),
            pltpu.VMEM((4, 64, ROWS), F32),
            pltpu.VMEM((4, 64, ROWS), F32),
            pltpu.VMEM((6, ROWS // 2, 128), BF),
            pltpu.VMEM((6, ROWS // 2, 128), BF),
            pltpu.VMEM((2, 128, ROWS), BF),
            pltpu.VMEM((2, 128, ROWS), BF),
            pltpu.VMEM((32, 32, 128), BF),
            pltpu.VMEM((32, SLOT, 128), BF),
            pltpu.VMEM((32, 32, 128), BF),
            pltpu.VMEM((32, SLOT, 128), BF),
            dma((3,)), dma((6,)),
            dma((8,)), dma((8,)),
            dma((8,)), dma((8,)),
            dma((8,)), dma((8,)),
            dma((2,)), dma((2,)),
            dma((2,)), dma((2,)),
            dma((2,)), dma((2,)),
        ],
        compiler_params=pltpu.CompilerParams(
            collective_id=0, has_side_effects=True, vmem_limit_bytes=56 * 2**20
        ),
    )(query, key_in, value, output, grad_out, log_sum_exp)


def solution(mesh):
    rows = P(("blk", "head"), None, None)
    return jax.shard_map(
        shards,
        mesh=mesh,
        in_specs=(rows,) * 5 + (P(None, None, ("blk", "head")),),
        out_specs=(rows,) * 3,
        check_vma=False,
    )
```

```python
import math
import jax
import jax.numpy as jnp
from jax import lax
from jax.experimental import pallas as pl
from jax.experimental.pallas import tpu as pltpu
from jax.sharding import PartitionSpec as P

BF, F32 = jnp.bfloat16, jnp.float32
MESH = pl.DeviceIdType.MESH
NT = (((1,), (1,)), ((), ()))
TN = (((0,), (0,)), ((), ()))
LOG2E = math.log2(math.e)
SCALE = 0.125
ROWS = 1024
SLOT = 64


def iota(shape, dim):
    return lax.broadcasted_iota(jnp.int32, shape, dim)


def low_half(rows):
    return iota((rows, 128), 1) < 64


def roll_half(tile):
    return pltpu.roll(tile, 64, 1)


def order_rows(transposed):
    shape = (128, 128)
    here, there = (iota(shape, 1), iota(shape, 0)) if transposed else (iota(shape, 0), iota(shape, 1))
    return jnp.where(there == 2 * lax.rem(here, 64) + lax.div(here, 64), 1.0, 0.0).astype(BF)


def eye(n):
    return jnp.where(iota((n, n), 0) == iota((n, n), 1), 1.0, 0.0).astype(BF)


def kernel(
    q_ref, k_ref, v_ref, o_ref, g_ref, lse_ref, iq, ikv,
    sq, sk, sa, qbuf, kbuf, ra, aux, qz, gz, qgt, kzt, vzt, dqa, dkt, dvt,
    sdq, rdq, skv, rkv, oq, okv,
    in_send, in_recv, ag_send, ag_recv, ax_send, ax_recv, dq_send, dq_recv,
    kx_send, kx_recv, dx_send, dx_recv, out_send, out_recv,
):
    blk, head = lax.axis_index("blk"), lax.axis_index("head")
    my_y, my_zl, my_c = lax.div(blk, 4), lax.rem(lax.div(blk, 2), 2), lax.rem(blk, 2)
    my_x, my_zh = lax.div(head, 4), lax.rem(head, 4)
    my_pair = my_x * 8 + my_y * 2 + my_zl

    def device(x, y, zl, zh, c):
        return (y * 4 + zl * 2 + c, x * 4 + zh)

    def offset(n):
        oy = lax.rem(lax.div(n, 2), 4)
        return lax.rem(lax.div(n, 8) + oy, 4), oy, lax.rem(n, 2)

    def ahead(n):
        ox, oy, ol = offset(n)
        return lax.rem(my_x + ox, 4), lax.rem(my_y + oy, 4), lax.rem(my_zl + ol, 2)

    def behind(n):
        ox, oy, ol = offset(n)
        return lax.rem(my_x + 4 - ox, 4), lax.rem(my_y + 4 - oy, 4), lax.rem(my_zl + 2 - ol, 2)

    def ring(distance):
        return device(my_x, my_y, my_zl, lax.rem(my_zh + distance, 4), my_c)

    partner = device(my_x, my_y, my_zl, my_zh, 1 - my_c)

    def send(src, dst, send_sem, recv_sem, target):
        return pltpu.make_async_remote_copy(
            src_ref=src, dst_ref=dst, send_sem=send_sem, recv_sem=recv_sem, device_id=target, device_id_type=MESH
        )

    def wait(ref, sem):
        pltpu.make_async_copy(ref, ref, sem).wait()

    barrier = pltpu.get_barrier_semaphore()

    def greet(n, c):
        x, y, zl = ahead(n)
        pl.semaphore_signal(barrier, inc=1, device_id=device(x, y, zl, my_zh, my_c), device_id_type=MESH)
        return c

    lax.fori_loop(1, 32, greet, 0)
    for target in (partner, ring(1), ring(2), ring(3)):
        pl.semaphore_signal(barrier, inc=1, device_id=target, device_id_type=MESH)

    to_seq = order_rows(False)

    def by_seq(ref):
        return jnp.dot(to_seq, ref[...].reshape(128, 1024), preferred_element_type=F32)

    def pack(low, high, dst):
        for t in range(8):
            a, b = low[:, t * 128:(t + 1) * 128], high[:, t * 128:(t + 1) * 128]
            even = jnp.where(low_half(128), a, roll_half(b)).astype(BF)
            odd = jnp.where(low_half(128), roll_half(a), b).astype(BF)
            for s in range(2):
                dst[4 * t + s] = even[s * 64:(s + 1) * 64]
                dst[4 * t + 2 + s] = odd[s * 64:(s + 1) * 64]

    grad_rows = by_seq(g_ref)
    pack(by_seq(q_ref), grad_rows, sq)
    rest = by_seq(o_ref) * grad_rows
    heads_of = jnp.where(iota((16, 1024), 0) == lax.div(iota((16, 1024), 1), 64), 1.0, 0.0).astype(BF)
    dots = jnp.zeros((16, 128), F32)
    for _ in range(3):
        part = rest.astype(BF)
        rest = rest - part.astype(F32)
        dots = dots + lax.dot_general(heads_of, part, NT, preferred_element_type=F32)
    dots_rolled = roll_half(dots)
    for h in range(16):
        for s in range(2):
            sa[2 * h + s, :, 0:64] = lse_ref[h, s:s + 1, :] * (-1.0 / SCALE)
            sa[2 * h + s, :, 64:128] = -(dots if s else dots_rolled)[h:h + 1, 64:128]
    pl.semaphore_wait(barrier, 35)

    def send_queries(n, c):
        x, y, zl = ahead(n)
        pair, target = x * 8 + y * 2 + zl, device(x, y, zl, my_zh, my_c)
        half, row = lax.div(n, 16), pl.multiple_of(lax.rem(n, 16) * SLOT, SLOT)
        send(sa.at[pair], ra.at[n], in_send.at[0], in_recv.at[half], target).start()
        send(sq.at[pair], qbuf.at[7 * half, pl.ds(row, SLOT)], in_send.at[1], in_recv.at[2 + half], target).start()
        return c

    def send_keys(n, c):
        x, y, zl = ahead(n)
        pair, target = x * 8 + y * 2 + zl, device(x, y, zl, my_zh, my_c)
        half, row = lax.div(n, 16), pl.multiple_of(lax.rem(n, 16) * SLOT, SLOT)
        send(sk.at[pair], kbuf.at[half, pl.ds(row, SLOT)], in_send.at[2], in_recv.at[4 + half], target).start()
        return c

    lax.fori_loop(1, 16, send_queries, 0)
    pack(by_seq(k_ref), by_seq(v_ref), sk)
    lax.fori_loop(1, 16, send_keys, 0)
    ra[0] = sa[my_pair]
    qbuf[0, 0:SLOT] = sq[my_pair]
    kbuf[0, 0:SLOT] = sk[my_pair]
    dqa[...] = jnp.zeros_like(dqa)
    dkt[...] = jnp.zeros_like(dkt)
    dvt[...] = jnp.zeros_like(dvt)

    def queries_here(half):
        first = 0 if half else 1
        wait(ra.at[pl.ds(16 * half + first, 16 - first)], in_recv.at[half])
        wait(qbuf.at[7 * half, pl.ds(0, (16 - first) * SLOT)], in_recv.at[2 + half])
        for m in range(8):
            a, b = ra[16 * half + 2 * m], ra[16 * half + 2 * m + 1]
            aux[7 * half, 0:1, m * 128:(m + 1) * 128] = jnp.where(low_half(1), a, roll_half(b))
            aux[7 * half, 1:2, m * 128:(m + 1) * 128] = jnp.where(low_half(1), roll_half(a), b)

    def pass_chunk(src, dst, distance):
        target = ring(distance)
        for buf, ss, rs in ((qbuf, ag_send, ag_recv), (aux, ax_send, ax_recv)):
            send(buf.at[src], buf.at[dst], ss.at[dst], rs.at[dst], target).start()

    def chunk_here(i):
        wait(qbuf.at[i], ag_recv.at[i])
        wait(aux.at[i], ax_recv.at[i])

    def prepare_keys(j):
        turned = lax.dot_general(eye(128), kbuf[j], NT, preferred_element_type=F32)
        row = iota((128, ROWS), 0)
        ones = jnp.where(lax.rem(row, 64) < 3, 1.0, 0.0)
        kzt[j] = jnp.where(row < 64, turned, ones).astype(BF)
        vzt[j] = jnp.where(row < 64, ones, turned).astype(BF)

    def prepare_queries(i):
        rest, parts = aux[i], []
        for _ in range(3):
            parts.append(rest.astype(BF).astype(F32))
            rest = rest - parts[-1]
        parts = jnp.concatenate(parts + [jnp.zeros((10, ROWS), F32)], 0).astype(BF)
        row, lane = iota((16, 128), 0), iota((16, 128), 1)
        spot = 64 * (1 - lax.rem(row, 2)) + lax.div(row, 2)
        spare = jnp.where((lane == spot) & (row < 6), 1.0, 0.0).astype(BF)
        columns = lax.dot_general(parts, spare, TN, preferred_element_type=F32).astype(BF)
        both = qbuf[i]
        low = low_half(ROWS)
        qz[...] = jnp.where(low, both, columns)
        gz[...] = jnp.where(low, columns, both)
        qgt[...] = lax.dot_general(eye(128), both, NT, preferred_element_type=F32).astype(BF)

    def front(j, part=slice(0, ROWS)):
        scores = jnp.dot(qz[...], kzt[j, :, part], preferred_element_type=F32)
        grad_probs = jnp.dot(gz[...], vzt[j, :, part], preferred_element_type=F32)
        probs = jnp.exp2(scores * (SCALE * LOG2E))
        return probs.astype(BF), (probs * grad_probs).astype(BF)

    def back(i, j, probs, grad_scores, part=slice(0, ROWS)):
        dvt[j, :, part] += jnp.dot(qgt[64:128], probs, preferred_element_type=F32)
        dkt[j, :, part] += jnp.dot(qgt[0:64], grad_scores, preferred_element_type=F32)
        dqa[i] += jnp.dot(grad_scores, kbuf[j, part], preferred_element_type=F32)

    def keys_here(j):
        if j < 2:
            first = 0 if j else 1
            wait(kbuf.at[j, pl.ds(0, (16 - first) * SLOT)], in_recv.at[4 + j])
            send(kbuf.at[j], kbuf.at[2 + j], kx_send.at[j], kx_recv.at[j], partner).start()
        else:
            wait(kbuf.at[j], kx_recv.at[j - 2])
        prepare_keys(j)

    def both_grads(j):
        return jnp.concatenate([dkt[j] * SCALE, dvt[j]], 0)

    def packed_queries(i):
        return jnp.where(low_half(ROWS // 2), dqa[i, 0:ROWS // 2], roll_half(dqa[i, ROWS // 2:ROWS]))

    def send_out(lo, hi, src, dst, which):
        def one(n, c):
            x, y, zl = behind(n)
            target = device(x, y, zl, my_zh, my_c)
            send(src.at[n], dst.at[my_pair], out_send.at[which], out_recv.at[which], target).start()
            return c

        lax.fori_loop(max(lo, 1), hi, one, 0)
        if lo == 0:
            dst[my_pair] = src[0]

    def finish_queries(half):
        total = packed_queries(7 * half)
        for i in (3, 5, 6) if half else (1, 2, 4):
            wait(rdq.at[i - 1], dq_recv.at[i])
            total = total + rdq[i - 1].astype(F32)
        total = total * SCALE
        low = low_half(32)
        for n in range(8):
            a, b = total[n * 64:n * 64 + 32], total[n * 64 + 32:n * 64 + 64]
            oq[16 * half + n] = jnp.where(low, a, roll_half(b)).astype(BF)
            oq[16 * half + 8 + n] = jnp.where(low, roll_half(a), b).astype(BF)
        send_out(16 * half, 16 * half + 16, oq, iq, 0)

    def finish_keys(j, part):
        total = jnp.concatenate([dkt[j, :, part] * SCALE, dvt[j, :, part]], 0) + rkv[j, :, part].astype(F32)
        total = lax.dot_general(total.astype(BF), eye(128), TN, preferred_element_type=F32).astype(BF)
        first = (ROWS * j + part.start) // SLOT
        count = (part.stop - part.start) // SLOT
        for n in range(count):
            okv[first + n] = total[n * SLOT:(n + 1) * SLOT]
        send_out(first, first + count, okv, ikv, 1)

    queries_here(0)
    pass_chunk(0, 1, 3)
    pass_chunk(0, 2, 1)
    keys_here(0)
    lax.fori_loop(16, 32, send_keys, 0)

    def start_turn(t, c):
        i, r = 7 * lax.div(t, 4), lax.rem(t, 4)
        second = lax.div(t, 4)
        j = (1 - second) * (lax.div(r, 2) + 2 * lax.rem(r, 2)) + second * (r + 2)

        @pl.when(t == 0)
        def _():
            prepare_queries(0)

        @pl.when(t == 1)
        def _():
            lax.fori_loop(16, 32, send_queries, 0)
            keys_here(2)

        @pl.when(t == 2)
        def _():
            keys_here(1)

        @pl.when(t == 3)
        def _():
            keys_here(3)

        @pl.when(t == 4)
        def _():
            queries_here(1)
            pass_chunk(7, 3, 3)
            pass_chunk(7, 6, 1)
            prepare_queries(7)

        back(i, j, *front(j))
        return c

    lax.fori_loop(0, 6, start_turn, 0)

    def middle_turn(i, c):
        @pl.when(i == 1)
        def _():
            chunk_here(1)
            pass_chunk(1, 4, 3)

        @pl.when(i == 2)
        def _():
            chunk_here(2)

        @pl.when(i == 3)
        def _():
            chunk_here(3)
            chunk_here(6)
            pass_chunk(6, 5, 1)

        for late in (4, 5):

            @pl.when(i == late)
            def _():
                chunk_here(late)

        prepare_queries(i)
        now = front(0)
        for j in range(4):
            later = front(j + 1) if j < 3 else None
            back(i, j, *now)
            now = later
        sdq[i - 1] = packed_queries(i).astype(BF)

        for done, distance in ((1, 1), (2, 3), (3, 1), (4, 2), (5, 2), (6, 3)):

            @pl.when(i == done)
            def _():
                send(sdq.at[done - 1], rdq.at[done - 1], dq_send.at[done], dq_recv.at[done], ring(distance)).start()

        return c

    lax.fori_loop(1, 7, middle_turn, 0)
    for half in range(2):
        skv[half] = both_grads(2 + half).astype(BF)
        send(skv.at[half], rkv.at[half], dx_send.at[half], dx_recv.at[half], partner).start()
    prepare_queries(7)
    finish_queries(0)

    for j in range(2):
        for part in (slice(0, ROWS // 2), slice(ROWS // 2, ROWS)):
            back(7, j, *front(j, part), part)
            if part.start == 0:
                wait(rkv.at[j], dx_recv.at[j])
            finish_keys(j, part)
    finish_queries(1)

    wait(sa.at[pl.ds(0, 31)], in_send.at[0])
    wait(sq.at[pl.ds(0, 31)], in_send.at[1])
    wait(sk.at[pl.ds(0, 31)], in_send.at[2])
    for i in range(1, 7):
        wait(qbuf.at[i], ag_send.at[i])
        wait(aux.at[i], ax_send.at[i])
        wait(sdq.at[i - 1], dq_send.at[i])
    for j in range(2):
        wait(kbuf.at[j], kx_send.at[j])
        wait(skv.at[j], dx_send.at[j])
    wait(oq.at[pl.ds(0, 31)], out_send.at[0])
    wait(okv.at[pl.ds(0, 31)], out_send.at[1])

    wait(ikv.at[pl.ds(0, 31)], out_recv.at[1])
    wait(iq.at[pl.ds(0, 31)], out_recv.at[0])


def unpack(iq, ikv, dq_ref, dk_ref, dv_ref):
    to_frames = order_rows(True)

    def interleave(tiles):
        rows = jnp.concatenate([jnp.concatenate([tiles(s, t) for t in range(8)], 1) for s in range(2)], 0)
        rows = jnp.dot(to_frames, rows.astype(BF), preferred_element_type=F32).astype(BF)
        return rows.reshape(64, 2, 1024)

    def key_tile(s, t):
        return jnp.where(low_half(64), ikv[4 * t + s].astype(F32), roll_half(ikv[4 * t + 2 + s].astype(F32)))

    def value_tile(s, t):
        return jnp.where(low_half(64), roll_half(ikv[4 * t + s].astype(F32)), ikv[4 * t + 2 + s].astype(F32))

    def query_tile(s, t):
        a, b = iq[4 * t + s].astype(F32), iq[4 * t + 2 + s].astype(F32)
        first = jnp.where(low_half(32), a, roll_half(b))
        second = jnp.where(low_half(32), roll_half(a), b)
        return jnp.concatenate([first, second], 0)

    dk_ref[...] = interleave(key_tile)
    dv_ref[...] = interleave(value_tile)
    dq_ref[...] = interleave(query_tile)


def shards(query, key_in, value, output, grad_out, log_sum_exp):
    dma = pltpu.SemaphoreType.DMA
    vmem = pl.BlockSpec(memory_space=pltpu.VMEM)
    back_here = [jax.ShapeDtypeStruct((32, 32, 128), BF), jax.ShapeDtypeStruct((32, SLOT, 128), BF)]
    parts = pl.pallas_call(
        kernel,
        out_shape=back_here,
        in_specs=[vmem] * 6,
        out_specs=[vmem] * 2,
        scratch_shapes=[
            pltpu.VMEM((32, SLOT, 128), BF),
            pltpu.VMEM((32, SLOT, 128), BF),
            pltpu.VMEM((32, 1, 128), F32),
            pltpu.VMEM((8, ROWS, 128), BF),
            pltpu.VMEM((4, ROWS, 128), BF),
            pltpu.VMEM((32, 1, 128), F32),
            pltpu.VMEM((8, 2, ROWS), F32),
            pltpu.VMEM((ROWS, 128), BF),
            pltpu.VMEM((ROWS, 128), BF),
            pltpu.VMEM((128, ROWS), BF),
            pltpu.VMEM((4, 128, ROWS), BF),
            pltpu.VMEM((4, 128, ROWS), BF),
            pltpu.VMEM((8, ROWS, 128), F32),
            pltpu.VMEM((4, 64, ROWS), F32),
            pltpu.VMEM((4, 64, ROWS), F32),
            pltpu.VMEM((6, ROWS // 2, 128), BF),
            pltpu.VMEM((6, ROWS // 2, 128), BF),
            pltpu.VMEM((2, 128, ROWS), BF),
            pltpu.VMEM((2, 128, ROWS), BF),
            pltpu.VMEM((32, 32, 128), BF),
            pltpu.VMEM((32, SLOT, 128), BF),
            dma((3,)), dma((6,)),
            dma((8,)), dma((8,)),
            dma((8,)), dma((8,)),
            dma((8,)), dma((8,)),
            dma((2,)), dma((2,)),
            dma((2,)), dma((2,)),
            dma((2,)), dma((2,)),
        ],
        compiler_params=pltpu.CompilerParams(
            collective_id=0, has_side_effects=True, vmem_limit_bytes=56 * 2**20
        ),
    )(query, key_in, value, output, grad_out, log_sum_exp)
    return pl.pallas_call(
        unpack,
        out_shape=[jax.ShapeDtypeStruct(query.shape, BF)] * 3,
        in_specs=[vmem] * 2,
        out_specs=[vmem] * 3,
    )(*parts)


def solution(mesh):
    rows = P(("blk", "head"), None, None)
    return jax.shard_map(
        shards,
        mesh=mesh,
        in_specs=(rows,) * 5 + (P(None, None, ("blk", "head")),),
        out_specs=(rows,) * 3,
        check_vma=False,
    )
```

```python
import math
import jax
import jax.numpy as jnp
from jax import lax
from jax.experimental import pallas as pl
from jax.experimental.pallas import tpu as pltpu
from jax.sharding import PartitionSpec as P

BF, F32 = jnp.bfloat16, jnp.float32
MESH = pl.DeviceIdType.MESH
NT = (((1,), (1,)), ((), ()))
TN = (((0,), (0,)), ((), ()))
LOG2E = math.log2(math.e)
SCALE = 0.125
ROWS = 1024
SLOT = 64


def iota(shape, dim):
    return lax.broadcasted_iota(jnp.int32, shape, dim)


def low_half(rows):
    return iota((rows, 128), 1) < 64


def roll_half(tile):
    return pltpu.roll(tile, 64, 1)


def order_rows(transposed):
    shape = (128, 128)
    here, there = (iota(shape, 1), iota(shape, 0)) if transposed else (iota(shape, 0), iota(shape, 1))
    return jnp.where(there == 2 * lax.rem(here, 64) + lax.div(here, 64), 1.0, 0.0).astype(BF)


def eye(n):
    return jnp.where(iota((n, n), 0) == iota((n, n), 1), 1.0, 0.0).astype(BF)


def kernel(
    q_ref, k_ref, v_ref, o_ref, g_ref, lse_ref, iq, ikv,
    sq, sk, sa, qbuf, kbuf, ra, aux, qz, gz, qgt, kzt, vzt, dqa, dkt, dvt,
    sdq, rdq, skv, rkv, oq, okv,
    in_send, in_recv, ag_send, ag_recv, ax_send, ax_recv, dq_send, dq_recv,
    kx_send, kx_recv, dx_send, dx_recv, out_send, out_recv,
):
    blk, head = lax.axis_index("blk"), lax.axis_index("head")
    my_y, my_zl, my_c = lax.div(blk, 4), lax.rem(lax.div(blk, 2), 2), lax.rem(blk, 2)
    my_x, my_zh = lax.div(head, 4), lax.rem(head, 4)
    my_pair = my_x * 8 + my_y * 2 + my_zl

    def device(x, y, zl, zh, c):
        return (y * 4 + zl * 2 + c, x * 4 + zh)

    def offset(n):
        oy = lax.rem(lax.div(n, 2), 4)
        return lax.rem(lax.div(n, 8) + oy, 4), oy, lax.rem(n, 2)

    def ahead(n):
        ox, oy, ol = offset(n)
        return lax.rem(my_x + ox, 4), lax.rem(my_y + oy, 4), lax.rem(my_zl + ol, 2)

    def behind(n):
        ox, oy, ol = offset(n)
        return lax.rem(my_x + 4 - ox, 4), lax.rem(my_y + 4 - oy, 4), lax.rem(my_zl + 2 - ol, 2)

    def ring(distance):
        return device(my_x, my_y, my_zl, lax.rem(my_zh + distance, 4), my_c)

    partner = device(my_x, my_y, my_zl, my_zh, 1 - my_c)

    def send(src, dst, send_sem, recv_sem, target):
        return pltpu.make_async_remote_copy(
            src_ref=src, dst_ref=dst, send_sem=send_sem, recv_sem=recv_sem, device_id=target, device_id_type=MESH
        )

    def wait(ref, sem):
        pltpu.make_async_copy(ref, ref, sem).wait()

    barrier = pltpu.get_barrier_semaphore()

    def greet(n, c):
        x, y, zl = ahead(n)
        pl.semaphore_signal(barrier, inc=1, device_id=device(x, y, zl, my_zh, my_c), device_id_type=MESH)
        return c

    lax.fori_loop(1, 32, greet, 0)
    for target in (partner, ring(1), ring(2), ring(3)):
        pl.semaphore_signal(barrier, inc=1, device_id=target, device_id_type=MESH)

    to_seq = order_rows(False)

    def by_seq(ref):
        return jnp.dot(to_seq, ref[...].reshape(128, 1024), preferred_element_type=F32)

    def pack(low, high, dst):
        for t in range(8):
            a, b = low[:, t * 128:(t + 1) * 128], high[:, t * 128:(t + 1) * 128]
            even = jnp.where(low_half(128), a, roll_half(b)).astype(BF)
            odd = jnp.where(low_half(128), roll_half(a), b).astype(BF)
            for s in range(2):
                dst[4 * t + s] = even[s * 64:(s + 1) * 64]
                dst[4 * t + 2 + s] = odd[s * 64:(s + 1) * 64]

    grad_rows = by_seq(g_ref)
    pack(by_seq(q_ref), grad_rows, sq)
    rest = by_seq(o_ref) * grad_rows
    heads_of = jnp.where(iota((16, 1024), 0) == lax.div(iota((16, 1024), 1), 64), 1.0, 0.0).astype(BF)
    dots = jnp.zeros((16, 128), F32)
    for _ in range(3):
        part = rest.astype(BF)
        rest = rest - part.astype(F32)
        dots = dots + lax.dot_general(heads_of, part, NT, preferred_element_type=F32)
    dots_rolled = roll_half(dots)
    for h in range(16):
        for s in range(2):
            sa[2 * h + s, :, 0:64] = lse_ref[h, s:s + 1, :] * (-1.0 / SCALE)
            sa[2 * h + s, :, 64:128] = -(dots if s else dots_rolled)[h:h + 1, 64:128]
    pl.semaphore_wait(barrier, 35)

    def send_queries(n, c):
        x, y, zl = ahead(n)
        pair, target = x * 8 + y * 2 + zl, device(x, y, zl, my_zh, my_c)
        half, row = lax.div(n, 16), pl.multiple_of(lax.rem(n, 16) * SLOT, SLOT)
        send(sa.at[pair], ra.at[n], in_send.at[0], in_recv.at[half], target).start()
        send(sq.at[pair], qbuf.at[7 * half, pl.ds(row, SLOT)], in_send.at[1], in_recv.at[2 + half], target).start()
        return c

    def send_keys(n, c):
        x, y, zl = ahead(n)
        pair, target = x * 8 + y * 2 + zl, device(x, y, zl, my_zh, my_c)
        half, row = lax.div(n, 16), pl.multiple_of(lax.rem(n, 16) * SLOT, SLOT)
        send(sk.at[pair], kbuf.at[half, pl.ds(row, SLOT)], in_send.at[2], in_recv.at[4 + half], target).start()
        return c

    lax.fori_loop(1, 16, send_queries, 0)
    pack(by_seq(k_ref), by_seq(v_ref), sk)
    lax.fori_loop(1, 16, send_keys, 0)
    ra[0] = sa[my_pair]
    qbuf[0, 0:SLOT] = sq[my_pair]
    kbuf[0, 0:SLOT] = sk[my_pair]
    dqa[...] = jnp.zeros_like(dqa)
    dkt[...] = jnp.zeros_like(dkt)
    dvt[...] = jnp.zeros_like(dvt)

    def queries_here(half):
        first = 0 if half else 1
        wait(ra.at[pl.ds(16 * half + first, 16 - first)], in_recv.at[half])
        wait(qbuf.at[7 * half, pl.ds(0, (16 - first) * SLOT)], in_recv.at[2 + half])
        for m in range(8):
            a, b = ra[16 * half + 2 * m], ra[16 * half + 2 * m + 1]
            aux[7 * half, 0:1, m * 128:(m + 1) * 128] = jnp.where(low_half(1), a, roll_half(b))
            aux[7 * half, 1:2, m * 128:(m + 1) * 128] = jnp.where(low_half(1), roll_half(a), b)

    def pass_chunk(src, dst, distance):
        target = ring(distance)
        for buf, ss, rs in ((qbuf, ag_send, ag_recv), (aux, ax_send, ax_recv)):
            send(buf.at[src], buf.at[dst], ss.at[dst], rs.at[dst], target).start()

    def chunk_here(i):
        wait(qbuf.at[i], ag_recv.at[i])
        wait(aux.at[i], ax_recv.at[i])

    def prepare_keys(j):
        turned = lax.dot_general(eye(128), kbuf[j], NT, preferred_element_type=F32)
        row = iota((128, ROWS), 0)
        ones = jnp.where(lax.rem(row, 64) < 3, 1.0, 0.0)
        kzt[j] = jnp.where(row < 64, turned, ones).astype(BF)
        vzt[j] = jnp.where(row < 64, ones, turned).astype(BF)

    def prepare_queries(i):
        rest, parts = aux[i], []
        for _ in range(3):
            parts.append(rest.astype(BF).astype(F32))
            rest = rest - parts[-1]
        parts = jnp.concatenate(parts + [jnp.zeros((10, ROWS), F32)], 0).astype(BF)
        row, lane = iota((16, 128), 0), iota((16, 128), 1)
        spot = 64 * (1 - lax.rem(row, 2)) + lax.div(row, 2)
        spare = jnp.where((lane == spot) & (row < 6), 1.0, 0.0).astype(BF)
        columns = lax.dot_general(parts, spare, TN, preferred_element_type=F32).astype(BF)
        both = qbuf[i]
        low = low_half(ROWS)
        qz[...] = jnp.where(low, both, columns)
        gz[...] = jnp.where(low, columns, both)
        qgt[...] = lax.dot_general(eye(128), both, NT, preferred_element_type=F32).astype(BF)

    def front(j, part=slice(0, ROWS)):
        scores = jnp.dot(qz[...], kzt[j, :, part], preferred_element_type=F32)
        grad_probs = jnp.dot(gz[...], vzt[j, :, part], preferred_element_type=F32)
        probs = jnp.exp2(scores * (SCALE * LOG2E))
        return probs.astype(BF), (probs * grad_probs).astype(BF)

    def back(i, j, probs, grad_scores, part=slice(0, ROWS)):
        dvt[j, :, part] += jnp.dot(qgt[64:128], probs, preferred_element_type=F32)
        dkt[j, :, part] += jnp.dot(qgt[0:64], grad_scores, preferred_element_type=F32)
        dqa[i] += jnp.dot(grad_scores, kbuf[j, part], preferred_element_type=F32)

    def keys_here(j):
        if j < 2:
            first = 0 if j else 1
            wait(kbuf.at[j, pl.ds(0, (16 - first) * SLOT)], in_recv.at[4 + j])
            send(kbuf.at[j], kbuf.at[2 + j], kx_send.at[j], kx_recv.at[j], partner).start()
        else:
            wait(kbuf.at[j], kx_recv.at[j - 2])
        prepare_keys(j)

    def both_grads(j):
        return jnp.concatenate([dkt[j] * SCALE, dvt[j]], 0)

    def packed_queries(i):
        return jnp.where(low_half(ROWS // 2), dqa[i, 0:ROWS // 2], roll_half(dqa[i, ROWS // 2:ROWS]))

    def send_out(lo, hi, src, dst, which):
        def one(n, c):
            x, y, zl = behind(n)
            target = device(x, y, zl, my_zh, my_c)
            send(src.at[n], dst.at[my_pair], out_send.at[which], out_recv.at[which], target).start()
            return c

        lax.fori_loop(max(lo, 1), hi, one, 0)
        if lo == 0:
            dst[my_pair] = src[0]

    def finish_queries(half):
        total = packed_queries(7 * half)
        for i in (3, 5, 6) if half else (1, 2, 4):
            wait(rdq.at[i - 1], dq_recv.at[i])
            total = total + rdq[i - 1].astype(F32)
        total = total * SCALE
        low = low_half(32)
        for n in range(8):
            a, b = total[n * 64:n * 64 + 32], total[n * 64 + 32:n * 64 + 64]
            oq[16 * half + n] = jnp.where(low, a, roll_half(b)).astype(BF)
            oq[16 * half + 8 + n] = jnp.where(low, roll_half(a), b).astype(BF)
        send_out(16 * half, 16 * half + 16, oq, iq, 0)

    def finish_keys(j, part):
        total = jnp.concatenate([dkt[j, :, part] * SCALE, dvt[j, :, part]], 0) + rkv[j, :, part].astype(F32)
        total = lax.dot_general(total.astype(BF), eye(128), TN, preferred_element_type=F32).astype(BF)
        first = (ROWS * j + part.start) // SLOT
        count = (part.stop - part.start) // SLOT
        for n in range(count):
            okv[first + n] = total[n * SLOT:(n + 1) * SLOT]
        send_out(first, first + count, okv, ikv, 1)

    queries_here(0)
    pass_chunk(0, 1, 3)
    pass_chunk(0, 2, 1)
    keys_here(0)
    lax.fori_loop(16, 32, send_keys, 0)

    def start_turn(t, c):
        j = lax.div(t, 2) + 2 * lax.rem(t, 2)

        @pl.when(t == 0)
        def _():
            prepare_queries(0)

        @pl.when(t == 1)
        def _():
            lax.fori_loop(16, 32, send_queries, 0)
            keys_here(2)

        @pl.when(t == 2)
        def _():
            keys_here(1)

        @pl.when(t == 3)
        def _():
            keys_here(3)

        back(0, j, *front(j))
        return c

    lax.fori_loop(0, 4, start_turn, 0)

    queries_here(1)
    pass_chunk(7, 3, 3)
    pass_chunk(7, 6, 1)
    prepare_queries(7)
    now, later = front(2), front(3)
    back(7, 2, *now)
    back(7, 3, *later)

    def middle_turn(i, c):
        @pl.when(i == 1)
        def _():
            chunk_here(1)
            pass_chunk(1, 4, 3)

        @pl.when(i == 2)
        def _():
            chunk_here(2)

        @pl.when(i == 3)
        def _():
            chunk_here(3)
            chunk_here(6)
            pass_chunk(6, 5, 1)

        for late in (4, 5):

            @pl.when(i == late)
            def _():
                chunk_here(late)

        prepare_queries(i)
        now = front(0)
        for j in range(4):
            later = front(j + 1) if j < 3 else None
            back(i, j, *now)
            now = later
        sdq[i - 1] = packed_queries(i).astype(BF)

        for done, distance in ((1, 1), (2, 3), (3, 1), (4, 2), (5, 2), (6, 3)):

            @pl.when(i == done)
            def _():
                send(sdq.at[done - 1], rdq.at[done - 1], dq_send.at[done], dq_recv.at[done], ring(distance)).start()

        return c

    lax.fori_loop(1, 7, middle_turn, 0)
    for half in range(2):
        skv[half] = both_grads(2 + half).astype(BF)
        send(skv.at[half], rkv.at[half], dx_send.at[half], dx_recv.at[half], partner).start()
    prepare_queries(7)
    finish_queries(0)

    for j in range(2):
        for part in (slice(0, ROWS // 2), slice(ROWS // 2, ROWS)):
            back(7, j, *front(j, part), part)
            if part.start == 0:
                wait(rkv.at[j], dx_recv.at[j])
            finish_keys(j, part)
    finish_queries(1)

    wait(sa.at[pl.ds(0, 31)], in_send.at[0])
    wait(sq.at[pl.ds(0, 31)], in_send.at[1])
    wait(sk.at[pl.ds(0, 31)], in_send.at[2])
    for i in range(1, 7):
        wait(qbuf.at[i], ag_send.at[i])
        wait(aux.at[i], ax_send.at[i])
        wait(sdq.at[i - 1], dq_send.at[i])
    for j in range(2):
        wait(kbuf.at[j], kx_send.at[j])
        wait(skv.at[j], dx_send.at[j])
    wait(oq.at[pl.ds(0, 31)], out_send.at[0])
    wait(okv.at[pl.ds(0, 31)], out_send.at[1])

    wait(ikv.at[pl.ds(0, 31)], out_recv.at[1])
    wait(iq.at[pl.ds(0, 31)], out_recv.at[0])


def unpack(iq, ikv, dq_ref, dk_ref, dv_ref):
    to_frames = order_rows(True)

    def interleave(tiles):
        rows = jnp.concatenate([jnp.concatenate([tiles(s, t) for t in range(8)], 1) for s in range(2)], 0)
        rows = jnp.dot(to_frames, rows.astype(BF), preferred_element_type=F32).astype(BF)
        return rows.reshape(64, 2, 1024)

    def key_tile(s, t):
        return jnp.where(low_half(64), ikv[4 * t + s].astype(F32), roll_half(ikv[4 * t + 2 + s].astype(F32)))

    def value_tile(s, t):
        return jnp.where(low_half(64), roll_half(ikv[4 * t + s].astype(F32)), ikv[4 * t + 2 + s].astype(F32))

    def query_tile(s, t):
        a, b = iq[4 * t + s].astype(F32), iq[4 * t + 2 + s].astype(F32)
        first = jnp.where(low_half(32), a, roll_half(b))
        second = jnp.where(low_half(32), roll_half(a), b)
        return jnp.concatenate([first, second], 0)

    dk_ref[...] = interleave(key_tile)
    dv_ref[...] = interleave(value_tile)
    dq_ref[...] = interleave(query_tile)


def shards(query, key_in, value, output, grad_out, log_sum_exp):
    dma = pltpu.SemaphoreType.DMA
    vmem = pl.BlockSpec(memory_space=pltpu.VMEM)
    back_here = [jax.ShapeDtypeStruct((32, 32, 128), BF), jax.ShapeDtypeStruct((32, SLOT, 128), BF)]
    parts = pl.pallas_call(
        kernel,
        out_shape=back_here,
        in_specs=[vmem] * 6,
        out_specs=[vmem] * 2,
        scratch_shapes=[
            pltpu.VMEM((32, SLOT, 128), BF),
            pltpu.VMEM((32, SLOT, 128), BF),
            pltpu.VMEM((32, 1, 128), F32),
            pltpu.VMEM((8, ROWS, 128), BF),
            pltpu.VMEM((4, ROWS, 128), BF),
            pltpu.VMEM((32, 1, 128), F32),
            pltpu.VMEM((8, 2, ROWS), F32),
            pltpu.VMEM((ROWS, 128), BF),
            pltpu.VMEM((ROWS, 128), BF),
            pltpu.VMEM((128, ROWS), BF),
            pltpu.VMEM((4, 128, ROWS), BF),
            pltpu.VMEM((4, 128, ROWS), BF),
            pltpu.VMEM((8, ROWS, 128), F32),
            pltpu.VMEM((4, 64, ROWS), F32),
            pltpu.VMEM((4, 64, ROWS), F32),
            pltpu.VMEM((6, ROWS // 2, 128), BF),
            pltpu.VMEM((6, ROWS // 2, 128), BF),
            pltpu.VMEM((2, 128, ROWS), BF),
            pltpu.VMEM((2, 128, ROWS), BF),
            pltpu.VMEM((32, 32, 128), BF),
            pltpu.VMEM((32, SLOT, 128), BF),
            dma((3,)), dma((6,)),
            dma((8,)), dma((8,)),
            dma((8,)), dma((8,)),
            dma((8,)), dma((8,)),
            dma((2,)), dma((2,)),
            dma((2,)), dma((2,)),
            dma((2,)), dma((2,)),
        ],
        compiler_params=pltpu.CompilerParams(
            collective_id=0, has_side_effects=True, vmem_limit_bytes=56 * 2**20
        ),
    )(query, key_in, value, output, grad_out, log_sum_exp)
    return pl.pallas_call(
        unpack,
        out_shape=[jax.ShapeDtypeStruct(query.shape, BF)] * 3,
        in_specs=[vmem] * 2,
        out_specs=[vmem] * 3,
    )(*parts)


def solution(mesh):
    rows = P(("blk", "head"), None, None)
    return jax.shard_map(
        shards,
        mesh=mesh,
        in_specs=(rows,) * 5 + (P(None, None, ("blk", "head")),),
        out_specs=(rows,) * 3,
        check_vma=False,
    )
```
